32 devices in a mesh: dp: 8 (over z, core), tensor: 4 (over y, x).
Axes of the slice: x: 2, y: 2, z: 4, core: 2. Of those that a mesh axis runs over, the one named last changes fastest.
Arguments:
- embeddings: bfloat16 [8192, 3584], P('dp'), may hold values from -6 to 6
- proj_weight: bfloat16 [3584, 1024], P(None, 'tensor'), may hold values from -0.09375 to 0.09375
- class_prior: float32 [8192, 512], P(('dp', 'tensor')), may hold values from 0.05 to 1
- seed_mask: int32 [8192], P(('dp', 'tensor')), may hold values 0 or 1
- nbr_block: int32 [32, 5], replicated, may hold values from 0 to 31, as said below
- nbr_cols: int32 [8192, 5, 8], P(('dp', 'tensor')), may hold values from 0 to 255
Outputs:
- labels: float32 [8192, 512], P(('dp', 'tensor'))
The draws below stay inside these ranges and needn't reach their ends.
Inputs may be any that keep to these rules, and one draw needn't show every extreme that they name: `nbr_block`: for row block b, the entries name blocks with the same remainder modulo 4 as b; the quotient by 4 equals that of b plus an offset modulo 8; the first entry's offset is +1, the others are distinct offsets drawn from -3, -2, -1, 2, 3, 4.
All inputs are finite; a program needn't handle non-finite values. No bound on the sum of `seed_mask` on one device may be relied on, other than what follows from the above.
Results may differ from the reference program's by a relative error of at most 0.0012.
Values may be sent and summed in bfloat16 or wider, within the bound.
A program may use at most 128 MiB of HBM per device.

```python
import jax
import jax.numpy as jnp
from jax import lax

D_IN = 3584
D_OUT = 1024
CLASSES = 512
BLK = 256
NB = 5
KS = 8
ITERS = 3
DP_GROUPS = 8
PANELS = 4
NBLK = 32
ROWS = 8192


def draw_nbr_block(key, part):
    other_offsets = jnp.array([-3, -2, -1, 2, 3, 4], dtype=jnp.int32)
    scores = jax.random.randint(key, (NBLK, 6), 0, 1 << 20) * 8 + jnp.arange(6, dtype=jnp.int32)[None, :]
    order = jnp.argsort(scores, axis=1)
    rest = jnp.take(other_offsets, order[:, :NB - 1])
    offsets = jnp.concatenate([jnp.ones((NBLK, 1), jnp.int32), rest], axis=1)
    blocks = jnp.arange(NBLK, dtype=jnp.int32)
    data_pos = blocks // PANELS
    tensor_pos = blocks % PANELS
    return ((data_pos[:, None] + offsets) % DP_GROUPS * PANELS + tensor_pos[:, None]).astype(jnp.int32)


def set_ends(values, own_key, low, high):
    longest = values.shape.index(max(values.shape))
    spots = []
    for shift in (0, 1):
        where = [jax.random.randint(jax.random.fold_in(own_key, axis), (), 0, length) for axis, length in enumerate(values.shape)]
        where[longest] = (where[longest] + shift) % values.shape[longest]
        spots.append(tuple(where))
    return values.at[spots[0]].set(low).at[spots[1]].set(high)


def level_of(rng, dims, pieces, low, top_value):
    level, own = 1.0, jax.random.fold_in(rng, 6)
    for axis_at, blocks in pieces:
        draws = jnp.exp(jax.random.uniform(jax.random.fold_in(own, axis_at), (blocks,), jnp.float32, low / len(pieces), top_value / len(pieces)))
        level = level * jnp.repeat(draws, dims[axis_at] // blocks).reshape([-1 if axis == axis_at else 1 for axis in range(len(dims))])
    return level


def gaussian(stream_key, extent, scale, bound, shards=(), held_as=jnp.bfloat16):
    result = jax.random.normal(stream_key, extent, jnp.float32) * scale
    if len(shards) > 0:
        result = level_of(stream_key, extent, shards, -0.22, 0.18) * result
    return jnp.clip(result, min=-bound, max=bound).astype(held_as)


def setup_inputs(seed: int = 0) -> dict:
    arg_keys = jax.random.split(jax.random.key(seed), 7)
    return {
        "embeddings": gaussian(arg_keys[0], (ROWS, D_IN), 1.0, 6.0, ((0, 8),)),
        "proj_weight": gaussian(arg_keys[1], (D_IN, D_OUT), D_IN ** -0.5, 0.09375, ((1, 4),)),
        "class_prior": jnp.clip(0.05 + 0.95 * jax.random.uniform(arg_keys[2], (ROWS, CLASSES), jnp.float32) ** level_of(arg_keys[2], (ROWS, CLASSES), ((0, 32),), -0.2, 0.2), 0.05, 1.0),
        "seed_mask": set_ends((jax.random.randint(arg_keys[3], (ROWS,), 0, 2) < 1).astype(jnp.int32), jax.random.fold_in(arg_keys[3], 1), 0, 1),
        "nbr_block": draw_nbr_block(jax.random.fold_in(arg_keys[6], 71), 0),
        "nbr_cols": set_ends(jax.random.randint(arg_keys[5], (ROWS, NB, KS), 0, BLK), jax.random.fold_in(arg_keys[5], 1), 0, BLK - 1).astype(jnp.int32),
    }


eps_norm = 1e-06
beta_scale = 16.0
alpha_keep = 0.8

def reference(embeddings, proj_weight, class_prior, seed_mask, nbr_block, nbr_cols):
    proj = jnp.dot(embeddings, proj_weight, preferred_element_type=jnp.float32).astype(jnp.bfloat16)
    proj_f = proj.astype(jnp.float32)
    unit = (proj_f * lax.rsqrt(lax.optimization_barrier(jnp.sum(proj_f * proj_f, axis=1, keepdims=True)) + eps_norm)).astype(jnp.bfloat16)
    unit_blocks = unit.reshape(NBLK, BLK, D_OUT)
    cols_blocks = nbr_cols.reshape(NBLK, BLK, NB, KS)
    column_ids = jnp.arange(BLK, dtype=jnp.int32)

    def block_affinity(packed):
        own_unit, own_list, own_cols = packed
        near_unit = jnp.take(unit_blocks, own_list, axis=0)
        tiles = jnp.einsum('id,sjd->sij', own_unit.astype(jnp.float32), near_unit.astype(jnp.float32))
        cols_slot = jnp.transpose(own_cols, (1, 0, 2))
        cosine = jnp.take_along_axis(tiles, cols_slot, axis=2)
        weight = jnp.exp(beta_scale * cosine)
        degree = lax.optimization_barrier(jnp.sum(weight, axis=(0, 2)))
        onehot = (cols_slot[..., None] == column_ids).astype(jnp.float32)
        affinity = lax.optimization_barrier(jnp.sum(weight[..., None] * onehot, axis=2)).astype(jnp.bfloat16)
        return (affinity, degree)
    affinity, degree = lax.map(block_affinity, (unit_blocks, nbr_block, cols_blocks))
    inv_root = lax.rsqrt(degree.reshape(ROWS))[:, None]
    seeds = seed_mask.astype(jnp.float32)[:, None] * class_prior / lax.optimization_barrier(jnp.mean(class_prior, axis=1, keepdims=True))
    labels = seeds
    for iteration in range(ITERS):
        scaled = (labels * inv_root).astype(jnp.bfloat16).reshape(NBLK, BLK, CLASSES)

        def block_spread(packed):
            own_aff, own_list = packed
            near_scaled = jnp.take(scaled, own_list, axis=0)
            return jnp.einsum('sij,sjc->ic', own_aff.astype(jnp.float32), near_scaled.astype(jnp.float32))
        spread = lax.map(block_spread, (affinity, nbr_block)).reshape(ROWS, CLASSES)
        labels = alpha_keep * inv_root * spread + (1.0 - alpha_keep) * seeds
    return labels
```

```python
import functools

import jax
import jax.numpy as jnp
from jax import lax
from jax.experimental import pallas as pl
from jax.experimental.pallas import tpu as pltpu
from jax.sharding import PartitionSpec as P

ITERS = 3
CHUNKS = 2
MESH = pl.DeviceIdType.MESH

eps_norm = 1e-06
beta_scale = 16.0
alpha_keep = 0.8


def as_column(row, count):
    return jnp.transpose(jnp.broadcast_to(row, (8, count)))[:, :1]


class Gather:
    def __init__(self, buf, send, recv, groups, me):
        self.buf, self.send, self.recv = buf, send, recv
        self.me, self.core, self.chip = me, lax.rem(me, 2), me // 2
        self.chips = groups // 2
        self.step_rows = buf.shape[1] // CHUNKS

    def copy(self, kind, slot, part, target):
        view = self.buf.at[slot, pl.ds(part * self.step_rows, self.step_rows)]
        return pltpu.make_async_remote_copy(
            src_ref=view,
            dst_ref=view,
            send_sem=self.send.at[kind, slot, part],
            recv_sem=self.recv.at[slot, part],
            device_id={"dp": target},
            device_id_type=MESH,
        )

    def up(self, slot, part):
        return self.copy(0, slot, part, lax.min(self.me + 2, 2 * self.chips - 2 + self.core))

    def down(self, slot, part):
        return self.copy(1, slot, part, lax.max(self.me - 2, self.core))

    def across(self, slot, part):
        return self.copy(2, slot, part, self.chip * 2 + 1 - self.core)

    def begin(self):
        for part in range(CHUNKS):
            @pl.when(self.chip < self.chips - 1)
            def _():
                self.up(self.me, part).start()

            @pl.when(self.chip > 0)
            def _():
                self.down(self.me, part).start()

            self.across(self.me, part).start()

    def from_below(self, dist):
        return self.chip - dist >= 0

    def from_above(self, dist):
        return self.chip + dist < self.chips

    def forward(self, dist):
        for part in range(CHUNKS):
            @pl.when(self.from_below(dist))
            def _():
                slot = self.me - 2 * dist
                self.across(slot, part).wait_recv()

                @pl.when(self.chip < self.chips - 1)
                def _():
                    self.up(slot, part).start()

                self.across(slot, part).start()

            @pl.when(self.from_above(dist))
            def _():
                slot = self.me + 2 * dist
                self.across(slot, part).wait_recv()

                @pl.when(self.chip > 0)
                def _():
                    self.down(slot, part).start()

                self.across(slot, part).start()

    def wait_other(self, slot):
        for part in range(CHUNKS):
            self.across(slot, part).wait_recv()

    def each(self, dist, use):
        for valid, chip in (
            (self.from_below(dist), self.chip - dist),
            (self.from_above(dist), self.chip + dist),
        ):
            @pl.when(valid)
            def _():
                if use is not None:
                    use(chip * 2 + self.core)
                other = chip * 2 + 1 - self.core
                self.wait_other(other)
                if use is not None:
                    use(other)

    def partner_block(self, use):
        other = self.chip * 2 + 1 - self.core
        self.wait_other(other)
        if use is not None:
            use(other)

    def drain(self):
        def one(chip, carry):
            slot = chip * 2 + self.core
            for part in range(CHUNKS):
                @pl.when((chip <= self.chip) & (self.chip < self.chips - 1))
                def _():
                    self.up(slot, part).wait_send()

                @pl.when((chip >= self.chip) & (self.chip > 0))
                def _():
                    self.down(slot, part).wait_send()

                self.across(slot, part).wait_send()
            return carry

        lax.fori_loop(0, self.chips, one, 0)


def kernel(
    groups, panels,
    emb_hbm, weight_hbm, prior_ref, mask_ref, nbr_ref, cols_ref,
    out_ref,
    emb, weight, made, panel, units, seed_blocks, scaled_a, scaled_b, roots, counts, aff, seeds, acc, degree,
    load_sem, a2a_send, a2a_recv, root_send, root_recv,
    u_send, u_recv, s_send, s_recv, a_send, a_recv, b_send, b_recv,
):
    me = lax.axis_index("dp")
    tensor = lax.axis_index("tensor")
    rows = prior_ref.shape[0]
    width = weight.shape[1]
    slots = cols_ref.shape[0]
    picks = cols_ref.shape[1]

    def panel_of(step):
        return lax.rem(tensor + step, panels)

    def load(step):
        span = pl.ds(pl.multiple_of(panel_of(step) * rows, rows), rows)
        return pltpu.make_async_copy(emb_hbm.at[span], emb.at[span], load_sem.at[step])

    weight_copy = pltpu.make_async_copy(weight_hbm, weight, load_sem.at[panels])
    weight_copy.start()
    for step in range(1, panels + 1):
        load(step % panels).start()

    barrier = pltpu.get_barrier_semaphore()
    for step in range(1, groups):
        pl.semaphore_signal(
            barrier, inc=1, device_id={"dp": lax.rem(me + step, groups)}, device_id_type=MESH
        )
    for step in range(1, panels):
        pl.semaphore_signal(barrier, inc=1, device_id={"tensor": panel_of(step)}, device_id_type=MESH)

    prior = prior_ref[...]
    mask = as_column(mask_ref[...].astype(jnp.float32), rows)
    seeds[...] = mask * prior / jnp.mean(prior, axis=1, keepdims=True)
    seed_blocks[me] = seeds[...].astype(jnp.bfloat16)
    pl.semaphore_wait(barrier, groups + panels - 2)

    seed_gather = Gather(seed_blocks, s_send, s_recv, groups, me)
    unit_gather = Gather(units, u_send, u_recv, groups, me)
    seed_gather.begin()

    def a2a(step):
        return pltpu.make_async_remote_copy(
            src_ref=made.at[step],
            dst_ref=panel.at[tensor],
            send_sem=a2a_send.at[step],
            recv_sem=a2a_recv.at[tensor],
            device_id={"tensor": panel_of(step)},
            device_id_type=MESH,
        )

    def project(step):
        load(step).wait()
        span = pl.ds(pl.multiple_of(panel_of(step) * rows, rows), rows)
        return jnp.dot(emb[span], weight[...], preferred_element_type=jnp.float32).astype(jnp.bfloat16)

    weight_copy.wait()

    def project_and_send(step, carry):
        made[step] = project(step)
        a2a(step).start()
        return carry

    lax.fori_loop(1, panels, project_and_send, 0)
    panel[tensor] = project(0)
    seed_gather.forward(1)
    for step in range(1, panels):
        source = panel_of(step)
        pltpu.make_async_remote_copy(
            src_ref=made.at[step],
            dst_ref=panel.at[source],
            send_sem=a2a_send.at[step],
            recv_sem=a2a_recv.at[source],
            device_id={"tensor": source},
            device_id_type=MESH,
        ).wait_recv()
    total = jnp.zeros((rows, 1), jnp.float32)
    for part in range(panels):
        values = panel[part].astype(jnp.float32)
        total += jnp.sum(values * values, axis=1, keepdims=True)
    scale = lax.rsqrt(total + eps_norm)
    for part in range(panels):
        units[me, :, part * width:(part + 1) * width] = (
            panel[part].astype(jnp.float32) * scale
        ).astype(jnp.bfloat16)
    unit_gather.begin()

    ids = lax.broadcasted_iota(jnp.int32, (rows, rows), 0)

    def count(slot, carry):
        chosen = jnp.zeros((picks, rows), jnp.int32) - 1
        for s in range(slots):
            match = (nbr_ref[me * panels + tensor, s] == slot * panels + tensor).astype(jnp.int32)
            chosen += match * (cols_ref[s] + 1)
        number = jnp.zeros((rows, rows), jnp.float32)
        for k in range(picks):
            number += jnp.where(ids == chosen[k:k + 1, :], 1.0, 0.0)
        counts[slot] = number
        return carry

    lax.fori_loop(0, groups, count, 0)
    degree[...] = jnp.zeros_like(degree)

    def seed_step(dist, carry):
        seed_gather.forward(dist)
        return carry

    lax.fori_loop(2, groups // 2, seed_step, 0)

    def affinity(slot):
        tile = lax.dot_general(
            units[slot], units[me], (((1,), (1,)), ((), ())), preferred_element_type=jnp.float32
        )
        number = counts[slot]
        grown = jnp.where(number > 0.0, number * jnp.exp(beta_scale * tile), 0.0)
        degree[...] += jnp.sum(grown, axis=0, keepdims=True)
        aff[slot] = jnp.transpose(grown).astype(jnp.bfloat16)

    unit_gather.partner_block(affinity)

    def unit_step(dist, carry):
        unit_gather.forward(dist)
        unit_gather.each(dist, affinity)
        return carry

    lax.fori_loop(1, groups // 2, unit_step, 0)

    root_row = lax.rsqrt(degree[...])
    roots[me] = jnp.broadcast_to(root_row, (8, rows))

    def root_copy(step, target, slot):
        return pltpu.make_async_remote_copy(
            src_ref=roots.at[slot],
            dst_ref=roots.at[slot],
            send_sem=root_send.at[step],
            recv_sem=root_recv.at[slot],
            device_id={"dp": target},
            device_id_type=MESH,
        )

    for step in range(1, groups):
        root_copy(step, lax.rem(me + step, groups), me).start()
    root = as_column(root_row, rows)
    seed_gather.partner_block(None)

    def seed_rest(dist, carry):
        seed_gather.each(dist, None)
        return carry

    lax.fori_loop(1, groups // 2, seed_rest, 0)
    acc[...] = jnp.zeros_like(acc)

    def first_spread(step, carry):
        slot = lax.rem(me + step, groups)
        root_copy(step, slot, slot).wait_recv()
        near = jnp.transpose(roots[slot])[:, :1]
        scaled = (seed_blocks[slot].astype(jnp.float32) * near).astype(jnp.bfloat16)
        acc[...] += jnp.dot(aff[slot], scaled, preferred_element_type=jnp.float32)
        return carry

    lax.fori_loop(1, groups, first_spread, 0)
    keep = alpha_keep * root

    gathers = []
    for held, send, recv in ((scaled_a, a_send, a_recv), (scaled_b, b_send, b_recv)):
        labels = keep * acc[...] + (1.0 - alpha_keep) * seeds[...]
        held[me] = (labels * root).astype(jnp.bfloat16)
        gather = Gather(held, send, recv, groups, me)
        gather.begin()
        gathers.append(gather)
        acc[...] = jnp.zeros_like(acc)

        def spread(slot, held=held):
            acc[...] += jnp.dot(aff[slot], held[slot], preferred_element_type=jnp.float32)

        gather.partner_block(spread)

        def label_step(dist, carry, gather=gather, spread=spread):
            gather.forward(dist)
            gather.each(dist, spread)
            return carry

        lax.fori_loop(1, groups // 2, label_step, 0)
    out_ref[...] = keep * acc[...] + (1.0 - alpha_keep) * seeds[...]

    for step in range(1, panels):
        a2a(step).wait_send()
    for step in range(1, groups):
        root_copy(step, lax.rem(me + step, groups), me).wait_send()
    for gather in (seed_gather, unit_gather, *gathers):
        gather.drain()


def body(embeddings, proj_weight, class_prior, seed_mask, nbr_block, nbr_cols):
    groups, panels = lax.axis_size("dp"), lax.axis_size("tensor")
    rows, classes = class_prior.shape
    depth, width = proj_weight.shape
    features = width * panels
    cols = jnp.transpose(nbr_cols, (1, 2, 0))
    vmem = pl.BlockSpec(memory_space=pltpu.VMEM)
    anywhere = pl.BlockSpec(memory_space=pl.ANY)
    dma = pltpu.SemaphoreType.DMA
    gather_sems = [dma((3, groups, CHUNKS)), dma((groups, CHUNKS))]
    return pl.pallas_call(
        functools.partial(kernel, groups, panels),
        out_shape=jax.ShapeDtypeStruct((rows, classes), jnp.float32),
        in_specs=[anywhere, anywhere, vmem, vmem, pl.BlockSpec(memory_space=pltpu.SMEM), vmem],
        out_specs=vmem,
        scratch_shapes=[
            pltpu.VMEM(embeddings.shape, jnp.bfloat16),
            pltpu.VMEM(proj_weight.shape, jnp.bfloat16),
            pltpu.VMEM((panels, rows, width), jnp.bfloat16),
            pltpu.VMEM((panels, rows, width), jnp.bfloat16),
            pltpu.VMEM((groups, rows, features), jnp.bfloat16),
            pltpu.VMEM((groups, rows, classes), jnp.bfloat16),
            pltpu.VMEM((groups, rows, classes), jnp.bfloat16),
            pltpu.VMEM((groups, rows, classes), jnp.bfloat16),
            pltpu.VMEM((groups, 8, rows), jnp.float32),
            pltpu.VMEM((groups, rows, rows), jnp.float32),
            pltpu.VMEM((groups, rows, rows), jnp.bfloat16),
            pltpu.VMEM((rows, classes), jnp.float32),
            pltpu.VMEM((rows, classes), jnp.float32),
            pltpu.VMEM((1, rows), jnp.float32),
            dma((panels + 1,)),
            dma((panels,)),
            dma((panels,)),
            dma((groups,)),
            dma((groups,)),
        ] + gather_sems * 4,
        compiler_params=pltpu.CompilerParams(
            collective_id=0, has_side_effects=True, vmem_limit_bytes=60 * 1024 * 1024
        ),
        cost_estimate=pl.CostEstimate(
            flops=2 * rows * panels * depth * width, bytes_accessed=10 << 20, transcendentals=0
        ),
    )(embeddings, proj_weight, class_prior, seed_mask.reshape(1, rows), nbr_block, cols)


def solution(mesh):
    return jax.shard_map(
        body,
        mesh=mesh,
        in_specs=(
            P("dp", None),
            P(None, "tensor"),
            P(("dp", "tensor"), None),
            P(("dp", "tensor")),
            P(),
            P(("dp", "tensor"), None, None),
        ),
        out_specs=P(("dp", "tensor"), None),
        check_vma=False,
    )
```

```python
import functools

import jax
import jax.numpy as jnp
from jax import lax
from jax.experimental import pallas as pl
from jax.experimental.pallas import tpu as pltpu
from jax.sharding import PartitionSpec as P

ITERS = 3
CHUNKS = 2
PIECES = 2
MESH = pl.DeviceIdType.MESH

eps_norm = 1e-06
beta_scale = 16.0
alpha_keep = 0.8


def as_column(row, count):
    return jnp.transpose(jnp.broadcast_to(row, (8, count)))[:, :1]


class Gather:
    def __init__(self, buf, send, recv, groups, me, inner, parts=CHUNKS):
        self.buf, self.send, self.recv, self.parts = buf, send, recv, parts
        self.me, self.core, self.chip = me, lax.rem(me, 2), me // 2
        self.chips = groups // 2
        self.inner = inner
        self.step_rows = buf.shape[1] // parts
        self.is_inner = (self.chip >= 1) & (self.chip <= self.chips - 2)
        self.can_up = self.chip <= self.chips - 3
        self.can_down = self.chip >= 2
        if inner:
            self.can_up = self.can_up & self.is_inner
            self.can_down = self.can_down & self.is_inner

    def copy(self, kind, slot, part, target):
        view = self.buf.at[slot, pl.ds(part * self.step_rows, self.step_rows)]
        return pltpu.make_async_remote_copy(
            src_ref=view,
            dst_ref=view,
            send_sem=self.send.at[kind, slot, part],
            recv_sem=self.recv.at[slot, part],
            device_id={"dp": target},
            device_id_type=MESH,
        )

    def up(self, slot, part):
        return self.copy(0, slot, part, lax.min(self.me + 2, 2 * self.chips - 2 + self.core))

    def down(self, slot, part):
        return self.copy(1, slot, part, lax.max(self.me - 2, self.core))

    def across(self, slot, part):
        return self.copy(2, slot, part, self.chip * 2 + 1 - self.core)

    def pass_on(self, slot, part, upward, downward):
        if upward:
            @pl.when(self.can_up)
            def _():
                self.up(slot, part).start()
        if downward:
            @pl.when(self.can_down)
            def _():
                self.down(slot, part).start()

        @pl.when(self.is_inner)
        def _():
            self.across(slot, part).start()

    def begin(self):
        for part in range(self.parts):
            self.pass_on(self.me, part, True, True)
        if self.inner:
            for part in range(self.parts):
                @pl.when(self.chip == 1)
                def _():
                    self.pass_on(self.me - 2, part, True, False)

                @pl.when(self.chip == self.chips - 2)
                def _():
                    self.pass_on(self.me + 2, part, False, True)

    def from_below(self, dist):
        return self.is_inner & (self.chip - dist >= 0)

    def from_above(self, dist):
        return self.is_inner & (self.chip + dist < self.chips)

    def arrives(self, dist):
        below, above = self.from_below(dist), self.from_above(dist)
        if self.inner:
            below = below & ((self.chip > 1) | (dist > 1))
            above = above & ((self.chip < self.chips - 2) | (dist > 1))
        return below, above

    def forward(self, dist):
        below, above = self.arrives(dist)
        for part in range(self.parts):
            @pl.when(below)
            def _():
                slot = self.me - 2 * dist
                self.across(slot, part).wait_recv()
                self.pass_on(slot, part, True, False)

            @pl.when(above)
            def _():
                slot = self.me + 2 * dist
                self.across(slot, part).wait_recv()
                self.pass_on(slot, part, False, True)

    def wait_other(self, slot):
        for part in range(self.parts):
            self.across(slot, part).wait_recv()

    def each(self, dist, use):
        for valid, chip in (
            (self.from_below(dist), self.chip - dist),
            (self.from_above(dist), self.chip + dist),
        ):
            @pl.when(valid)
            def _():
                if use is not None:
                    use(chip * 2 + self.core)
                other = chip * 2 + 1 - self.core
                self.wait_other(other)
                if use is not None:
                    use(other)

    def own_chip(self, use):
        @pl.when(self.is_inner)
        def _():
            other = self.chip * 2 + 1 - self.core
            if use is not None:
                use(self.me)
            self.wait_other(other)
            if use is not None:
                use(other)

    def receive(self, use, begin=1):
        self.own_chip(use)

        def step(dist, carry):
            self.forward(dist)
            self.each(dist, use)
            return carry

        lax.fori_loop(begin, self.chips - 1, step, 0)

    def drain(self):
        def one(chip, carry):
            slot = chip * 2 + self.core
            for part in range(self.parts):
                @pl.when((chip <= self.chip) & self.can_up)
                def _():
                    self.up(slot, part).wait_send()

                @pl.when((chip >= self.chip) & self.can_down)
                def _():
                    self.down(slot, part).wait_send()

                @pl.when(self.is_inner)
                def _():
                    self.across(slot, part).wait_send()
            return carry

        lax.fori_loop(0, self.chips, one, 0)


def kernel(
    groups, panels,
    emb_hbm, weight_hbm, prior_ref, mask_ref, nbr_ref, cols_ref,
    out_ref,
    emb, weight, made, panel, units, seed_blocks, scaled_a, scaled_b, roots, counts, aff, seeds, acc, degree,
    far_cols, back,
    load_sem, a2a_send, a2a_recv, far_send, far_recv, back_send, back_recv,
    u_send, u_recv, s_send, s_recv, a_send, a_recv, b_send, b_recv, r_send, r_recv,
):
    me = lax.axis_index("dp")
    tensor = lax.axis_index("tensor")
    rows = prior_ref.shape[0]
    width = weight.shape[1]
    slots = cols_ref.shape[0]
    picks = cols_ref.shape[1]

    def panel_of(step):
        return lax.rem(tensor + step, panels)

    def load(step):
        span = pl.ds(pl.multiple_of(panel_of(step) * rows, rows), rows)
        return pltpu.make_async_copy(emb_hbm.at[span], emb.at[span], load_sem.at[step])

    weight_copy = pltpu.make_async_copy(weight_hbm, weight, load_sem.at[panels])
    weight_copy.start()
    for step in range(1, panels + 1):
        load(step % panels).start()

    barrier = pltpu.get_barrier_semaphore()
    for step in range(1, groups):
        pl.semaphore_signal(
            barrier, inc=1, device_id={"dp": lax.rem(me + step, groups)}, device_id_type=MESH
        )
    for step in range(1, panels):
        pl.semaphore_signal(barrier, inc=1, device_id={"tensor": panel_of(step)}, device_id_type=MESH)

    prior = prior_ref[...]
    mask = as_column(mask_ref[...].astype(jnp.float32), rows)
    seeds[...] = mask * prior / jnp.mean(prior, axis=1, keepdims=True)
    seed_blocks[me] = seeds[...].astype(jnp.bfloat16)
    pl.semaphore_wait(barrier, groups + panels - 2)

    chip, chips, core = me // 2, groups // 2, lax.rem(me, 2)
    is_inner = (chip >= 1) & (chip <= chips - 2)
    is_outer = (chip == 0) | (chip == chips - 1)
    has_far = (chip == 1) | (chip == chips - 2)
    partner = jnp.where(chip == 0, 2 + core, 2 * chips - 4 + core)
    far = jnp.where(chip == 1, core, 2 * chips - 2 + core)

    seed_gather = Gather(seed_blocks, s_send, s_recv, groups, me, False)
    unit_gather = Gather(units, u_send, u_recv, groups, me, False)
    cols_copy = pltpu.make_async_remote_copy(
        src_ref=cols_ref,
        dst_ref=far_cols,
        send_sem=far_send,
        recv_sem=far_recv,
        device_id={"dp": partner},
        device_id_type=MESH,
    )

    @pl.when(is_outer)
    def _():
        cols_copy.start()

    seed_gather.begin()

    def a2a(step):
        return pltpu.make_async_remote_copy(
            src_ref=made.at[step],
            dst_ref=panel.at[tensor],
            send_sem=a2a_send.at[step],
            recv_sem=a2a_recv.at[tensor],
            device_id={"tensor": panel_of(step)},
            device_id_type=MESH,
        )

    def project(step):
        load(step).wait()
        span = pl.ds(pl.multiple_of(panel_of(step) * rows, rows), rows)
        return jnp.dot(emb[span], weight[...], preferred_element_type=jnp.float32).astype(jnp.bfloat16)

    weight_copy.wait()

    def project_and_send(step, carry):
        made[step] = project(step)
        a2a(step).start()
        return carry

    lax.fori_loop(1, panels, project_and_send, 0)
    panel[tensor] = project(0)
    seed_gather.forward(1)
    for step in range(1, panels):
        source = panel_of(step)
        pltpu.make_async_remote_copy(
            src_ref=made.at[step],
            dst_ref=panel.at[source],
            send_sem=a2a_send.at[step],
            recv_sem=a2a_recv.at[source],
            device_id={"tensor": source},
            device_id_type=MESH,
        ).wait_recv()
    total = jnp.zeros((rows, 1), jnp.float32)
    for part in range(panels):
        values = panel[part].astype(jnp.float32)
        total += jnp.sum(values * values, axis=1, keepdims=True)
    scale = lax.rsqrt(total + eps_norm)
    for part in range(panels):
        units[me, :, part * width:(part + 1) * width] = (
            panel[part].astype(jnp.float32) * scale
        ).astype(jnp.bfloat16)
    unit_gather.begin()

    ids = lax.broadcasted_iota(jnp.int32, (rows, rows), 0)

    def owners(use):
        use(0, me, cols_ref)

        @pl.when(has_far)
        def _():
            use(1, far, far_cols)

    def count_for(which, owner, cols):
        def count(slot, carry):
            chosen = jnp.zeros((picks, rows), jnp.int32) - 1
            for s in range(slots):
                match = (nbr_ref[owner * panels + tensor, s] == slot * panels + tensor).astype(jnp.int32)
                chosen += match * (cols[s] + 1)
            number = jnp.zeros((rows, rows), jnp.float32)
            for k in range(picks):
                number += jnp.where(ids == chosen[k:k + 1, :], 1.0, 0.0)
            counts[which, slot] = number
            return carry

        lax.fori_loop(0, groups, count, 0)

    seed_gather.forward(2)

    @pl.when(is_inner)
    def _():
        @pl.when(has_far)
        def _():
            cols_copy.wait_recv()

        owners(count_for)

    degree[...] = jnp.zeros_like(degree)

    def seed_step(dist, carry):
        seed_gather.forward(dist)
        return carry

    lax.fori_loop(3, chips - 1, seed_step, 0)

    def affinity(slot):
        def one(which, owner, cols):
            tile = lax.dot_general(
                units[slot], units[owner], (((1,), (1,)), ((), ())), preferred_element_type=jnp.float32
            )
            number = counts[which, slot]
            grown = jnp.where(number > 0.0, number * jnp.exp(beta_scale * tile), 0.0)
            degree[which] += jnp.sum(grown, axis=0, keepdims=True)
            aff[which, slot] = jnp.transpose(grown).astype(jnp.bfloat16)

        owners(one)

    unit_gather.forward(1)
    unit_gather.own_chip(affinity)
    unit_gather.each(1, affinity)

    def unit_step(dist, carry):
        unit_gather.forward(dist)
        unit_gather.each(dist, affinity)
        return carry

    lax.fori_loop(2, chips - 1, unit_step, 0)
    gathers = [seed_gather, unit_gather]

    def seed_rest(dist, carry):
        seed_gather.each(dist, None)
        return carry

    seed_gather.own_chip(None)
    lax.fori_loop(1, chips - 1, seed_rest, 0)

    def column_of(slot):
        return jnp.transpose(roots[slot])[:, :1]

    def add_spread(slot, near, first, width):
        def one(which, owner, cols):
            acc[which, :, first:first + width] += jnp.dot(
                aff[which, slot], near, preferred_element_type=jnp.float32
            )

        owners(one)

    @pl.when(is_inner)
    def _():
        def set_root(which, owner, cols):
            roots[owner] = jnp.broadcast_to(lax.rsqrt(degree[which]), (8, rows))

        owners(set_root)

    root_gather = Gather(roots, r_send, r_recv, groups, me, True, 1)
    root_gather.begin()
    gathers.append(root_gather)
    acc[...] = jnp.zeros_like(acc)
    classes = prior_ref.shape[1]

    def first_spread(slot):
        scaled = (seed_blocks[slot].astype(jnp.float32) * column_of(slot)).astype(jnp.bfloat16)
        add_spread(slot, scaled, 0, classes)

    root_gather.receive(first_spread)

    def mix(first, width):
        def one(which, owner, cols):
            root = column_of(owner)
            if which == 0:
                kept = seeds[:, first:first + width]
            else:
                kept = seed_blocks[owner, :, first:first + width].astype(jnp.float32)
            labels = alpha_keep * root * acc[which, :, first:first + width] + (1.0 - alpha_keep) * kept
            held[owner] = (labels * root).astype(jnp.bfloat16)

        owners(one)

    held = scaled_a
    pl.when(is_inner)(lambda: mix(0, classes))
    acc[...] = jnp.zeros_like(acc)
    gather = Gather(scaled_a, a_send, a_recv, groups, me, True)
    gather.begin()
    gathers.append(gather)
    gather.receive(lambda slot: add_spread(slot, scaled_a[slot], 0, classes))

    piece = classes // PIECES
    last = []
    for part in range(PIECES):
        held = scaled_b.at[part]
        pl.when(is_inner)(lambda: mix(part * piece, piece))
        gather = Gather(held, b_send.at[part], b_recv.at[part], groups, me, True)
        gather.begin()
        last.append(gather)
    gathers += last
    acc[...] = jnp.zeros_like(acc)

    def back_copy(part, target):
        return pltpu.make_async_remote_copy(
            src_ref=back.at[part],
            dst_ref=back.at[part],
            send_sem=back_send.at[part],
            recv_sem=back_recv.at[part],
            device_id={"dp": target},
            device_id_type=MESH,
        )

    for part in range(PIECES):
        near_blocks = scaled_b.at[part]
        last[part].receive(lambda slot: add_spread(slot, near_blocks[slot], part * piece, piece))

        @pl.when(has_far)
        def _():
            back[part] = alpha_keep * column_of(far) * acc[1, :, part * piece:(part + 1) * piece]
            back_copy(part, far).start()

        @pl.when(is_inner)
        def _():
            back_kept = alpha_keep * column_of(me) * acc[0, :, part * piece:(part + 1) * piece]
            out_ref[:, part * piece:(part + 1) * piece] = (
                back_kept + (1.0 - alpha_keep) * seeds[:, part * piece:(part + 1) * piece]
            )

        @pl.when(is_outer)
        def _():
            back_copy(part, partner).wait_recv()
            out_ref[:, part * piece:(part + 1) * piece] = (
                back[part] + (1.0 - alpha_keep) * seeds[:, part * piece:(part + 1) * piece]
            )

    @pl.when(is_outer)
    def _():
        cols_copy.wait_send()

    @pl.when(has_far)
    def _():
        for part in range(PIECES):
            back_copy(part, far).wait_send()

    for step in range(1, panels):
        a2a(step).wait_send()
    for gather in gathers:
        gather.drain()


def body(embeddings, proj_weight, class_prior, seed_mask, nbr_block, nbr_cols):
    groups, panels = lax.axis_size("dp"), lax.axis_size("tensor")
    rows, classes = class_prior.shape
    depth, width = proj_weight.shape
    features = width * panels
    cols = jnp.transpose(nbr_cols, (1, 2, 0))
    vmem = pl.BlockSpec(memory_space=pltpu.VMEM)
    anywhere = pl.BlockSpec(memory_space=pl.ANY)
    dma = pltpu.SemaphoreType.DMA
    gather_sems = [dma((3, groups, CHUNKS)), dma((groups, CHUNKS))]
    return pl.pallas_call(
        functools.partial(kernel, groups, panels),
        out_shape=jax.ShapeDtypeStruct((rows, classes), jnp.float32),
        in_specs=[anywhere, anywhere, vmem, vmem, pl.BlockSpec(memory_space=pltpu.SMEM), vmem],
        out_specs=vmem,
        scratch_shapes=[
            pltpu.VMEM(embeddings.shape, jnp.bfloat16),
            pltpu.VMEM(proj_weight.shape, jnp.bfloat16),
            pltpu.VMEM((panels, rows, width), jnp.bfloat16),
            pltpu.VMEM((panels, rows, width), jnp.bfloat16),
            pltpu.VMEM((groups, rows, features), jnp.bfloat16),
            pltpu.VMEM((groups, rows, classes), jnp.bfloat16),
            pltpu.VMEM((groups, rows, classes), jnp.bfloat16),
            pltpu.VMEM((PIECES, groups, rows, classes // PIECES), jnp.bfloat16),
            pltpu.VMEM((groups, 8, rows), jnp.float32),
            pltpu.VMEM((2, groups, rows, rows), jnp.float32),
            pltpu.VMEM((2, groups, rows, rows), jnp.bfloat16),
            pltpu.VMEM((rows, classes), jnp.float32),
            pltpu.VMEM((2, rows, classes), jnp.float32),
            pltpu.VMEM((2, 1, rows), jnp.float32),
            pltpu.VMEM(cols.shape, jnp.int32),
            pltpu.VMEM((PIECES, rows, classes // PIECES), jnp.float32),
            dma((panels + 1,)),
            dma((panels,)),
            dma((panels,)),
            dma(()),
            dma(()),
            dma((PIECES,)),
            dma((PIECES,)),
        ] + gather_sems * 3 + [
            dma((PIECES, 3, groups, CHUNKS)),
            dma((PIECES, groups, CHUNKS)),
            dma((3, groups, 1)),
            dma((groups, 1)),
        ],
        compiler_params=pltpu.CompilerParams(
            collective_id=0, has_side_effects=True, vmem_limit_bytes=60 * 1024 * 1024
        ),
        cost_estimate=pl.CostEstimate(
            flops=2 * rows * panels * depth * width, bytes_accessed=10 << 20, transcendentals=0
        ),
    )(embeddings, proj_weight, class_prior, seed_mask.reshape(1, rows), nbr_block, cols)


def solution(mesh):
    return jax.shard_map(
        body,
        mesh=mesh,
        in_specs=(
            P("dp", None),
            P(None, "tensor"),
            P(("dp", "tensor"), None),
            P(("dp", "tensor")),
            P(),
            P(("dp", "tensor"), None, None),
        ),
        out_specs=P(("dp", "tensor"), None),
        check_vma=False,
    )
```

```python
import functools

import jax
import jax.numpy as jnp
from jax import lax
from jax.experimental import pallas as pl
from jax.experimental.pallas import tpu as pltpu
from jax.sharding import PartitionSpec as P

ITERS = 3
CHUNKS = 2
PIECES = 2
MESH = pl.DeviceIdType.MESH

eps_norm = 1e-06
beta_scale = 16.0
alpha_keep = 0.8


def as_column(row, count):
    return jnp.transpose(jnp.broadcast_to(row, (8, count)))[:, :1]


class Gather:
    def __init__(self, buf, send, recv, groups, me, inner, parts=CHUNKS):
        self.buf, self.send, self.recv, self.parts = buf, send, recv, parts
        self.me, self.core, self.chip = me, lax.rem(me, 2), me // 2
        self.chips = groups // 2
        self.inner = inner
        self.step_rows = buf.shape[1] // parts
        self.is_inner = (self.chip >= 1) & (self.chip <= self.chips - 2)
        self.can_up = self.chip <= self.chips - 3
        self.can_down = self.chip >= 2
        if inner:
            self.can_up = self.can_up & self.is_inner
            self.can_down = self.can_down & self.is_inner

    def copy(self, kind, slot, part, target):
        view = self.buf.at[slot, pl.ds(part * self.step_rows, self.step_rows)]
        return pltpu.make_async_remote_copy(
            src_ref=view,
            dst_ref=view,
            send_sem=self.send.at[kind, slot, part],
            recv_sem=self.recv.at[slot, part],
            device_id={"dp": target},
            device_id_type=MESH,
        )

    def up(self, slot, part):
        return self.copy(0, slot, part, lax.min(self.me + 2, 2 * self.chips - 2 + self.core))

    def down(self, slot, part):
        return self.copy(1, slot, part, lax.max(self.me - 2, self.core))

    def across(self, slot, part):
        return self.copy(2, slot, part, self.chip * 2 + 1 - self.core)

    def pass_on(self, slot, part, upward, downward):
        if upward:
            @pl.when(self.can_up)
            def _():
                self.up(slot, part).start()
        if downward:
            @pl.when(self.can_down)
            def _():
                self.down(slot, part).start()

        @pl.when(self.is_inner)
        def _():
            self.across(slot, part).start()

    def begin(self):
        for part in range(self.parts):
            self.pass_on(self.me, part, True, True)
        if self.inner:
            for part in range(self.parts):
                @pl.when(self.chip == 1)
                def _():
                    self.pass_on(self.me - 2, part, True, False)

                @pl.when(self.chip == self.chips - 2)
                def _():
                    self.pass_on(self.me + 2, part, False, True)

    def from_below(self, dist):
        return self.is_inner & (self.chip - dist >= 0)

    def from_above(self, dist):
        return self.is_inner & (self.chip + dist < self.chips)

    def arrives(self, dist):
        below, above = self.from_below(dist), self.from_above(dist)
        if self.inner:
            below = below & ((self.chip > 1) | (dist > 1))
            above = above & ((self.chip < self.chips - 2) | (dist > 1))
        return below, above

    def forward(self, dist):
        below, above = self.arrives(dist)
        for part in range(self.parts):
            @pl.when(below)
            def _():
                slot = self.me - 2 * dist
                self.across(slot, part).wait_recv()
                self.pass_on(slot, part, True, False)

            @pl.when(above)
            def _():
                slot = self.me + 2 * dist
                self.across(slot, part).wait_recv()
                self.pass_on(slot, part, False, True)

    def wait_other(self, slot):
        for part in range(self.parts):
            self.across(slot, part).wait_recv()

    def each(self, dist, use):
        for valid, chip in (
            (self.from_below(dist), self.chip - dist),
            (self.from_above(dist), self.chip + dist),
        ):
            @pl.when(valid)
            def _():
                if use is not None:
                    use(chip * 2 + self.core)
                other = chip * 2 + 1 - self.core
                self.wait_other(other)
                if use is not None:
                    use(other)

    def own_chip(self, use):
        @pl.when(self.is_inner)
        def _():
            other = self.chip * 2 + 1 - self.core
            if use is not None:
                use(self.me)
            self.wait_other(other)
            if use is not None:
                use(other)

    def receive(self, use, begin=1):
        self.own_chip(use)

        def step(dist, carry):
            self.forward(dist)
            self.each(dist, use)
            return carry

        lax.fori_loop(begin, self.chips - 1, step, 0)

    def drain(self):
        def one(chip, carry):
            slot = chip * 2 + self.core
            for part in range(self.parts):
                @pl.when((chip <= self.chip) & self.can_up)
                def _():
                    self.up(slot, part).wait_send()

                @pl.when((chip >= self.chip) & self.can_down)
                def _():
                    self.down(slot, part).wait_send()

                @pl.when(self.is_inner)
                def _():
                    self.across(slot, part).wait_send()
            return carry

        lax.fori_loop(0, self.chips, one, 0)


def kernel(
    groups, panels,
    emb_hbm, weight_hbm, prior_ref, mask_ref, nbr_ref, cols_ref,
    out_ref,
    emb, weight, made, panel, units, seed_blocks, scaled_a, scaled_b, roots, counts, aff, seeds, acc, degree,
    far_cols, back,
    load_sem, a2a_send, a2a_recv, far_send, far_recv, back_send, back_recv,
    u_send, u_recv, s_send, s_recv, a_send, a_recv, b_send, b_recv, r_send, r_recv,
):
    me = lax.axis_index("dp")
    tensor = lax.axis_index("tensor")
    rows = prior_ref.shape[0]
    width = weight.shape[1]
    slots = cols_ref.shape[0]
    picks = cols_ref.shape[1]

    def panel_of(step):
        return lax.rem(tensor + step, panels)

    def load(step):
        span = pl.ds(pl.multiple_of(panel_of(step) * rows, rows), rows)
        return pltpu.make_async_copy(emb_hbm.at[span], emb.at[span], load_sem.at[step])

    weight_copy = pltpu.make_async_copy(weight_hbm, weight, load_sem.at[panels])
    weight_copy.start()
    for step in range(1, panels + 1):
        load(step % panels).start()

    barrier = pltpu.get_barrier_semaphore()
    for step in range(1, groups):
        pl.semaphore_signal(
            barrier, inc=1, device_id={"dp": lax.rem(me + step, groups)}, device_id_type=MESH
        )
    for step in range(1, panels):
        pl.semaphore_signal(barrier, inc=1, device_id={"tensor": panel_of(step)}, device_id_type=MESH)

    prior = prior_ref[...]
    mask = as_column(mask_ref[...].astype(jnp.float32), rows)
    seeds[...] = mask * prior / jnp.mean(prior, axis=1, keepdims=True)
    seed_blocks[me] = seeds[...].astype(jnp.bfloat16)
    pl.semaphore_wait(barrier, groups + panels - 2)

    chip, chips, core = me // 2, groups // 2, lax.rem(me, 2)
    is_inner = (chip >= 1) & (chip <= chips - 2)
    is_outer = (chip == 0) | (chip == chips - 1)
    has_far = (chip == 1) | (chip == chips - 2)
    partner = jnp.where(chip == 0, 2 + core, 2 * chips - 4 + core)
    far = jnp.where(chip == 1, core, 2 * chips - 2 + core)

    seed_gather = Gather(seed_blocks, s_send, s_recv, groups, me, False)
    unit_gather = Gather(units, u_send, u_recv, groups, me, False)
    cols_copy = pltpu.make_async_remote_copy(
        src_ref=cols_ref,
        dst_ref=far_cols,
        send_sem=far_send,
        recv_sem=far_recv,
        device_id={"dp": partner},
        device_id_type=MESH,
    )

    @pl.when(is_outer)
    def _():
        cols_copy.start()

    seed_gather.begin()

    def a2a(step):
        return pltpu.make_async_remote_copy(
            src_ref=made.at[step],
            dst_ref=panel.at[tensor],
            send_sem=a2a_send.at[step],
            recv_sem=a2a_recv.at[tensor],
            device_id={"tensor": panel_of(step)},
            device_id_type=MESH,
        )

    def project(step):
        load(step).wait()
        span = pl.ds(pl.multiple_of(panel_of(step) * rows, rows), rows)
        return jnp.dot(emb[span], weight[...], preferred_element_type=jnp.float32).astype(jnp.bfloat16)

    weight_copy.wait()

    def project_and_send(step, carry):
        made[step] = project(step)
        a2a(step).start()
        return carry

    lax.fori_loop(1, panels, project_and_send, 0)
    panel[tensor] = project(0)
    seed_gather.forward(1)
    for step in range(1, panels):
        source = panel_of(step)
        pltpu.make_async_remote_copy(
            src_ref=made.at[step],
            dst_ref=panel.at[source],
            send_sem=a2a_send.at[step],
            recv_sem=a2a_recv.at[source],
            device_id={"tensor": source},
            device_id_type=MESH,
        ).wait_recv()
    total = jnp.zeros((rows, 1), jnp.float32)
    for part in range(panels):
        values = panel[part].astype(jnp.float32)
        total += jnp.sum(values * values, axis=1, keepdims=True)
    scale = lax.rsqrt(total + eps_norm)
    for part in range(panels):
        units[me, :, part * width:(part + 1) * width] = (
            panel[part].astype(jnp.float32) * scale
        ).astype(jnp.bfloat16)
    unit_gather.begin()

    ids = lax.broadcasted_iota(jnp.int32, (rows, rows), 0)

    def owners(use):
        use(0, me, cols_ref)

        @pl.when(has_far)
        def _():
            use(1, far, far_cols)

    def count_for(which, owner, cols):
        def count(slot, carry):
            chosen = jnp.zeros((picks, rows), jnp.int32) - 1
            for s in range(slots):
                match = (nbr_ref[owner * panels + tensor, s] == slot * panels + tensor).astype(jnp.int32)
                chosen += match * (cols[s] + 1)
            number = jnp.zeros((rows, rows), jnp.float32)
            for k in range(picks):
                number += jnp.where(ids == chosen[k:k + 1, :], 1.0, 0.0)
            counts[which, slot] = number
            return carry

        lax.fori_loop(0, groups, count, 0)

    seed_gather.forward(2)

    @pl.when(is_inner)
    def _():
        @pl.when(has_far)
        def _():
            cols_copy.wait_recv()

        owners(count_for)

    degree[...] = jnp.zeros_like(degree)

    def seed_step(dist, carry):
        seed_gather.forward(dist)
        return carry

    lax.fori_loop(3, chips - 1, seed_step, 0)

    def affinity(slot):
        def one(which, owner, cols):
            tile = lax.dot_general(
                units[slot], units[owner], (((1,), (1,)), ((), ())), preferred_element_type=jnp.float32
            )
            number = counts[which, slot]
            grown = jnp.where(number > 0.0, number * jnp.exp(beta_scale * tile), 0.0)
            degree[which] += jnp.sum(grown, axis=0, keepdims=True)
            aff[which, slot] = jnp.transpose(grown).astype(jnp.bfloat16)

        owners(one)

    unit_gather.forward(1)
    unit_gather.own_chip(affinity)
    unit_gather.each(1, affinity)

    def unit_step(dist, carry):
        unit_gather.forward(dist)
        unit_gather.each(dist, affinity)
        return carry

    lax.fori_loop(2, chips - 1, unit_step, 0)
    gathers = [seed_gather, unit_gather]

    def seed_rest(dist, carry):
        seed_gather.each(dist, None)
        return carry

    seed_gather.own_chip(None)
    lax.fori_loop(1, chips - 1, seed_rest, 0)

    def column_of(slot):
        return jnp.transpose(roots[slot])[:, :1]

    def add_spread(slot, near, first, width):
        def one(which, owner, cols):
            acc[which, :, first:first + width] += jnp.dot(
                aff[which, slot], near, preferred_element_type=jnp.float32
            )

        owners(one)

    @pl.when(is_inner)
    def _():
        def set_root(which, owner, cols):
            roots[owner] = jnp.broadcast_to(lax.rsqrt(degree[which]), (8, rows))

        owners(set_root)

    root_gather = Gather(roots, r_send, r_recv, groups, me, True, 1)
    root_gather.begin()
    gathers.append(root_gather)
    acc[...] = jnp.zeros_like(acc)
    classes = prior_ref.shape[1]

    piece = classes // PIECES

    def mix(first, width, held):
        def one(which, owner, cols):
            root = column_of(owner)
            if which == 0:
                kept = seeds[:, first:first + width]
            else:
                kept = seed_blocks[owner, :, first:first + width].astype(jnp.float32)
            labels = alpha_keep * root * acc[which, :, first:first + width] + (1.0 - alpha_keep) * kept
            held[owner] = (labels * root).astype(jnp.bfloat16)
            acc[which, :, first:first + width] = jnp.zeros((rows, width), jnp.float32)

        owners(one)

    def send_piece(part, blocks, send, recv):
        held = blocks.at[part]
        pl.when(is_inner)(lambda: mix(part * piece, piece, held))
        gather = Gather(held, send.at[part], recv.at[part], groups, me, True)
        gather.begin()
        gathers.append(gather)
        return gather

    second = []
    for part in range(PIECES):
        span = slice(part * piece, (part + 1) * piece)

        def first_spread(slot):
            scaled = (seed_blocks[slot, :, span].astype(jnp.float32) * column_of(slot)).astype(jnp.bfloat16)
            add_spread(slot, scaled, part * piece, piece)

        if part == 0:
            root_gather.receive(first_spread)
        else:
            @pl.when(is_inner)
            def _():
                def rest(slot, carry):
                    first_spread(slot)
                    return carry

                lax.fori_loop(0, groups, rest, 0)
        second.append(send_piece(part, scaled_a, a_send, a_recv))
    last = []
    for part in range(PIECES):
        near_blocks = scaled_a.at[part]
        second[part].receive(lambda slot: add_spread(slot, near_blocks[slot], part * piece, piece))
        last.append(send_piece(part, scaled_b, b_send, b_recv))

    def back_copy(part, target):
        return pltpu.make_async_remote_copy(
            src_ref=back.at[part],
            dst_ref=back.at[part],
            send_sem=back_send.at[part],
            recv_sem=back_recv.at[part],
            device_id={"dp": target},
            device_id_type=MESH,
        )

    for part in range(PIECES):
        near_blocks = scaled_b.at[part]
        last[part].receive(lambda slot: add_spread(slot, near_blocks[slot], part * piece, piece))

        @pl.when(has_far)
        def _():
            back[part] = alpha_keep * column_of(far) * acc[1, :, part * piece:(part + 1) * piece]
            back_copy(part, far).start()

        @pl.when(is_inner)
        def _():
            back_kept = alpha_keep * column_of(me) * acc[0, :, part * piece:(part + 1) * piece]
            out_ref[:, part * piece:(part + 1) * piece] = (
                back_kept + (1.0 - alpha_keep) * seeds[:, part * piece:(part + 1) * piece]
            )

        @pl.when(is_outer)
        def _():
            back_copy(part, partner).wait_recv()
            out_ref[:, part * piece:(part + 1) * piece] = (
                back[part] + (1.0 - alpha_keep) * seeds[:, part * piece:(part + 1) * piece]
            )

    @pl.when(is_outer)
    def _():
        cols_copy.wait_send()

    @pl.when(has_far)
    def _():
        for part in range(PIECES):
            back_copy(part, far).wait_send()

    for step in range(1, panels):
        a2a(step).wait_send()
    for gather in gathers:
        gather.drain()


def body(embeddings, proj_weight, class_prior, seed_mask, nbr_block, nbr_cols):
    groups, panels = lax.axis_size("dp"), lax.axis_size("tensor")
    rows, classes = class_prior.shape
    depth, width = proj_weight.shape
    features = width * panels
    cols = jnp.transpose(nbr_cols, (1, 2, 0))
    vmem = pl.BlockSpec(memory_space=pltpu.VMEM)
    anywhere = pl.BlockSpec(memory_space=pl.ANY)
    dma = pltpu.SemaphoreType.DMA
    gather_sems = [dma((3, groups, CHUNKS)), dma((groups, CHUNKS))]
    return pl.pallas_call(
        functools.partial(kernel, groups, panels),
        out_shape=jax.ShapeDtypeStruct((rows, classes), jnp.float32),
        in_specs=[anywhere, anywhere, vmem, vmem, pl.BlockSpec(memory_space=pltpu.SMEM), vmem],
        out_specs=vmem,
        scratch_shapes=[
            pltpu.VMEM(embeddings.shape, jnp.bfloat16),
            pltpu.VMEM(proj_weight.shape, jnp.bfloat16),
            pltpu.VMEM((panels, rows, width), jnp.bfloat16),
            pltpu.VMEM((panels, rows, width), jnp.bfloat16),
            pltpu.VMEM((groups, rows, features), jnp.bfloat16),
            pltpu.VMEM((groups, rows, classes), jnp.bfloat16),
            pltpu.VMEM((PIECES, groups, rows, classes // PIECES), jnp.bfloat16),
            pltpu.VMEM((PIECES, groups, rows, classes // PIECES), jnp.bfloat16),
            pltpu.VMEM((groups, 8, rows), jnp.float32),
            pltpu.VMEM((2, groups, rows, rows), jnp.float32),
            pltpu.VMEM((2, groups, rows, rows), jnp.bfloat16),
            pltpu.VMEM((rows, classes), jnp.float32),
            pltpu.VMEM((2, rows, classes), jnp.float32),
            pltpu.VMEM((2, 1, rows), jnp.float32),
            pltpu.VMEM(cols.shape, jnp.int32),
            pltpu.VMEM((PIECES, rows, classes // PIECES), jnp.float32),
            dma((panels + 1,)),
            dma((panels,)),
            dma((panels,)),
            dma(()),
            dma(()),
            dma((PIECES,)),
            dma((PIECES,)),
        ] + gather_sems * 2 + [
            dma((PIECES, 3, groups, CHUNKS)),
            dma((PIECES, groups, CHUNKS)),
            dma((PIECES, 3, groups, CHUNKS)),
            dma((PIECES, groups, CHUNKS)),
            dma((3, groups, 1)),
            dma((groups, 1)),
        ],
        compiler_params=pltpu.CompilerParams(
            collective_id=0, has_side_effects=True, vmem_limit_bytes=60 * 1024 * 1024
        ),
        cost_estimate=pl.CostEstimate(
            flops=2 * rows * panels * depth * width, bytes_accessed=10 << 20, transcendentals=0
        ),
    )(embeddings, proj_weight, class_prior, seed_mask.reshape(1, rows), nbr_block, cols)


def solution(mesh):
    return jax.shard_map(
        body,
        mesh=mesh,
        in_specs=(
            P("dp", None),
            P(None, "tensor"),
            P(("dp", "tensor"), None),
            P(("dp", "tensor")),
            P(),
            P(("dp", "tensor"), None, None),
        ),
        out_specs=P(("dp", "tensor"), None),
        check_vma=False,
    )
```
